32 devices in a mesh: groups: 2 (over x), seq: 8 (over z, y), chan: 2 (over core).
Axes of the slice: x: 2, y: 2, z: 4, core: 2. Of those that a mesh axis runs over, the one named last changes fastest.
Arguments:
- tower_input: bfloat16 [16384, 1536], P(('groups', 'seq'), 'chan'), parts along dimension 0, may hold values from -6 to 6
- dna_bases: int32 [16384, 32], P(('groups', 'seq')), parts along dimension 0, may hold values from 0 to 3
- base_embed: bfloat16 [128, 1536], P(None, 'chan'), may hold values from -1 to 1
- in_scale: float32 [2, 1536], P(None, 'chan'), may hold values from 0.5 to 1.5
- entry_norm_shift: float32 [2, 1536], P(None, 'chan'), may hold values from -0.5 to 0.5
- conv_w: bfloat16 [2, 3, 1536, 768], P(None, None, 'chan'), may hold values from -0.09375 to 0.09375
- mid_scale: float32 [2, 768], P(None, 'chan'), may hold values from 0.5 to 1.5
- mid_shift: float32 [2, 768], P(None, 'chan'), may hold values from -0.5 to 0.5
- point_w: bfloat16 [2, 768, 1536], P(None, None, 'chan'), may hold values from -0.21875 to 0.21875
- pooling_weight: bfloat16 [1536, 1536], P(None, 'chan'), may hold values from -0.15625 to 0.15625
Outputs:
- pooled: bfloat16 [8192, 1536], P(('groups', 'seq'), 'chan'), parts along dimension 0
The draws below stay inside these ranges and needn't reach their ends.
There are 2 independent parts, one for each index of `groups`. The reference program is written for one: setup_inputs(seed, part) draws one part's arguments, and reference() takes and returns one part's arrays. A program takes and returns all parts, laid end to end along the dimension named above; an argument that names none is the same for every part. Nothing has to cross between parts.
All inputs are finite; a program needn't handle non-finite values.
Results may differ from the reference program's by a relative error of at most 0.018.
Values may be sent and summed in bfloat16 or wider, within the bound.
A program may use at most 128 MiB of HBM per device.

```python
import jax
import jax.numpy as jnp

C = 1536
B = 768
BASES = 32
NBLK = 2
FIRST_SPACING = 32
SECOND_SPACING = 48
BINS = 8192


def touch_ends(values, own_key, low, top_value):
    index_at = [jax.random.randint(jax.random.fold_in(own_key, axis), (), 0, length) for axis, length in enumerate(values.shape)]
    main_axis = values.shape.index(max(values.shape))
    neighbour = index_at[:main_axis] + [(index_at[main_axis] + 1) % values.shape[main_axis]] + index_at[main_axis + 1:]
    return values.at[tuple(index_at)].set(low).at[tuple(neighbour)].set(top_value)


def shard_levels(rng, extent, cuts, least, top_value):
    factor_of = 1.0
    for dim, blocks in cuts:
        draws = jax.random.uniform(jax.random.fold_in(jax.random.fold_in(rng, 6), dim), (blocks,), jnp.float32, least / len(cuts), top_value / len(cuts))
        factor_of = factor_of * jnp.repeat(jnp.exp(draws), extent[dim] // blocks).reshape((-1,) + (1,) * (len(extent) - 1 - dim))
    return factor_of


def scatter_about(key, shape, deviation, limit, shards=(), held_as=jnp.bfloat16):
    entries = deviation * jax.random.normal(key, shape, jnp.float32)
    if shards:
        entries = entries * shard_levels(key, shape, shards, -0.22, 0.18)
    return jnp.clip(entries, -limit, limit).astype(held_as)


def setup_inputs(seed: int = 0, part: int = 0) -> dict:
    keys = jax.random.split(jax.random.key(seed), 11)
    part_keys = jax.random.split(jax.random.fold_in(keys[10], part), 11)
    tower_input = scatter_about(part_keys[0], (BINS, C), 1.0, 6.0, ((0, 8), (1, 2)))
    dna_bases = touch_ends(jax.random.randint(part_keys[1], (BINS, BASES), 0, 4), jax.random.fold_in(part_keys[1], 1), 0, 3).astype(jnp.int32)
    base_embed = scatter_about(keys[2], (4 * BASES, C), BASES ** -0.5, 1.0, ((1, 2),))
    in_scale = jnp.clip(1.0 + 0.1 * jax.random.normal(keys[3], (NBLK, C), jnp.float32), 0.5, 1.5)
    entry_norm_shift = jnp.clip(jax.random.uniform(keys[4], (NBLK, C), jnp.float32, -0.5, 0.5) * shard_levels(keys[4], (NBLK, C), ((1, 2),), -0.4, 0.0), -0.5, 0.5)
    conv_w = scatter_about(keys[5], (NBLK, 3, C, B), (3 * C) ** -0.5, 0.09375, ((2, 2),))
    mid_scale = jnp.clip(1.0 + 0.1 * jax.random.normal(keys[6], (NBLK, B), jnp.float32), 0.5, 1.5)
    mid_shift = jnp.clip(jax.random.uniform(keys[7], (NBLK, B), jnp.float32, -0.5, 0.5) * shard_levels(keys[7], (NBLK, B), ((1, 2),), -0.4, 0.0), -0.5, 0.5)
    point_w = scatter_about(keys[8], (NBLK, B, C), B ** -0.5, 0.21875, ((2, 2),))
    pooling_weight = scatter_about(keys[9], (C, C), C ** -0.5, 0.15625, ((1, 2),))
    return dict(tower_input=tower_input, dna_bases=dna_bases, base_embed=base_embed, in_scale=in_scale, entry_norm_shift=entry_norm_shift, conv_w=conv_w, mid_scale=mid_scale, mid_shift=mid_shift, point_w=point_w, pooling_weight=pooling_weight)


def gelu_tanh(value):
    return jax.nn.gelu(value, approximate=True)


def reference(tower_input, dna_bases, base_embed, in_scale, entry_norm_shift, conv_w, mid_scale, mid_shift, point_w, pooling_weight):
    length = tower_input.shape[0]
    onehot = (dna_bases[:, :, None] == jnp.arange(4, dtype=jnp.int32)[None, None, :]).astype(jnp.bfloat16)
    onehot = onehot.reshape(length, 4 * BASES)
    stream = (tower_input.astype(jnp.float32) + jnp.dot(onehot, base_embed, preferred_element_type=jnp.float32)).astype(jnp.bfloat16)
    spacing_list = (FIRST_SPACING, SECOND_SPACING)
    for layer_idx in range(NBLK):
        spread = spacing_list[layer_idx]
        act = gelu_tanh(stream.astype(jnp.float32) * in_scale[layer_idx] + entry_norm_shift[layer_idx]).astype(jnp.bfloat16)
        padded = jnp.pad(act, ((spread, spread), (0, 0)))
        partial_value = jnp.dot(padded[0:length], conv_w[layer_idx, 0], preferred_element_type=jnp.float32)
        partial_value = partial_value + jnp.dot(act, conv_w[layer_idx, 1], preferred_element_type=jnp.float32)
        partial_value = partial_value + jnp.dot(padded[2 * spread:2 * spread + length], conv_w[layer_idx, 2], preferred_element_type=jnp.float32)
        inner = gelu_tanh(partial_value * mid_scale[layer_idx] + mid_shift[layer_idx]).astype(jnp.bfloat16)
        update = jnp.dot(inner, point_w[layer_idx], preferred_element_type=jnp.float32)
        stream = (stream.astype(jnp.float32) + update).astype(jnp.bfloat16)
    score_logits = jnp.dot(stream, pooling_weight, preferred_element_type=jnp.float32)
    width = stream.shape[1]
    pairs = stream.astype(jnp.float32).reshape(length // 2, 2, width)
    logit_pairs = score_logits.reshape(length // 2, 2, width)
    weight_first = jax.nn.sigmoid(logit_pairs[:, 0] - logit_pairs[:, 1])
    result = pairs[:, 1] + weight_first * (pairs[:, 0] - pairs[:, 1])
    return result.astype(jnp.bfloat16)
```

```python
import functools

import jax
import jax.numpy as jnp
from jax import lax
from jax.experimental import pallas as pl
from jax.experimental.pallas import tpu as pltpu
from jax.sharding import PartitionSpec as P

SPACINGS = (32, 48)
PAD = 48
CHUNKS = 4
LANES = 128
MESH = pl.DeviceIdType.MESH
F32 = jnp.float32
BF16 = jnp.bfloat16
GELU_A = 0.7978845608028654
GELU_B = 0.7978845608028654 * 0.044715


def gelu(v):
    half = 0.5 * v
    return half + half * jnp.tanh(v * (GELU_A + GELU_B * (v * v)))


def dot(a, b):
    return jnp.dot(a, b, preferred_element_type=F32)


def kernel(
    seq_count,
    tower_h,
    bases_h,
    embed_h,
    scale_h,
    shift_h,
    conv_h,
    mid_scale_h,
    mid_shift_h,
    point_h,
    pool_h,
    out_h,
    tower,
    bases,
    embed,
    scale,
    shift,
    conv,
    mids,
    point,
    pool,
    stream,
    padded0,
    padded1,
    sent,
    got,
    final,
    diff_sent,
    diff_got,
    result,
    load_sem,
    conv_sem,
    mid_sem,
    halo_send,
    halo_recv,
    part_send,
    part_recv,
    diff_send,
    diff_recv,
    out_sem,
):
    seq = lax.axis_index("seq")
    me = lax.axis_index("chan")
    other = 1 - me
    rows, width = tower.shape
    step = rows // CHUNKS
    half = step // 2
    padded = (padded0, padded1)

    loads = {}

    def load(name, src, dst, sem):
        copy = pltpu.make_async_copy(src, dst, sem)
        copy.start()
        loads[name] = copy

    load("bases", bases_h, bases, load_sem.at[0])
    load("embed", embed_h, embed, load_sem.at[1])
    load("tower", tower_h, tower, load_sem.at[2])
    load("scale", scale_h, scale, load_sem.at[3])
    load("shift", shift_h, shift, load_sem.at[4])
    load("mid0", mid_scale_h, mids.at[me, 0], load_sem.at[5])
    load("mid1", mid_shift_h, mids.at[me, 1], load_sem.at[6])
    for layer in range(2):
        for tap in range(3):
            load(
                ("conv", layer, tap),
                conv_h.at[layer, tap],
                conv.at[layer, pl.ds(tap * width, width)],
                conv_sem.at[3 * layer + tap],
            )
        load(("point", layer), point_h.at[layer], point.at[layer], load_sem.at[7 + layer])
    load("pool0", pool_h.at[pl.ds(pl.multiple_of(me * width, width), width)], pool.at[0], load_sem.at[9])
    load("pool1", pool_h.at[pl.ds(pl.multiple_of(other * width, width), width)], pool.at[1], load_sem.at[10])

    edge = jnp.zeros((PAD, width), BF16)
    for buffer in padded:
        buffer[0:PAD] = edge
        buffer[PAD + rows : PAD + rows + PAD] = edge

    barrier = pltpu.get_barrier_semaphore()
    pl.semaphore_signal(barrier, inc=1, device_id={"chan": other}, device_id_type=MESH)

    @pl.when(seq > 0)
    def _():
        pl.semaphore_signal(barrier, inc=1, device_id={"seq": seq - 1}, device_id_type=MESH)

    @pl.when(seq < seq_count - 1)
    def _():
        pl.semaphore_signal(barrier, inc=1, device_id={"seq": seq + 1}, device_id_type=MESH)

    def to_right(layer):
        d = SPACINGS[layer]
        return pltpu.make_async_remote_copy(
            src_ref=padded[layer].at[pl.ds(PAD + rows - d, d)],
            dst_ref=padded[layer].at[pl.ds(PAD - d, d)],
            send_sem=halo_send.at[2 * layer],
            recv_sem=halo_recv.at[2 * layer],
            device_id={"seq": seq + 1},
            device_id_type=MESH,
        )

    def to_left(layer):
        d = SPACINGS[layer]
        return pltpu.make_async_remote_copy(
            src_ref=padded[layer].at[pl.ds(PAD, d)],
            dst_ref=padded[layer].at[pl.ds(PAD + rows, d)],
            send_sem=halo_send.at[2 * layer + 1],
            recv_sem=halo_recv.at[2 * layer + 1],
            device_id={"seq": seq - 1},
            device_id_type=MESH,
        )

    def send_right(layer):
        @pl.when(seq < seq_count - 1)
        def _():
            to_right(layer).start()

    def send_left(layer):
        @pl.when(seq > 0)
        def _():
            to_left(layer).start()

    def wait_left_rim(layer):
        @pl.when(seq > 0)
        def _():
            to_right(layer).wait_recv()

    def wait_right_rim(layer):
        @pl.when(seq < seq_count - 1)
        def _():
            to_left(layer).wait_recv()

    def mid_copy(which):
        return pltpu.make_async_remote_copy(
            src_ref=mids.at[me, which],
            dst_ref=mids.at[me, which],
            send_sem=mid_sem.at[which],
            recv_sem=mid_sem.at[2 + which],
            device_id={"chan": other},
            device_id_type=MESH,
        )

    def part_copy(layer, c):
        return pltpu.make_async_remote_copy(
            src_ref=sent.at[layer, pl.ds(c * step, step)],
            dst_ref=got.at[layer, pl.ds(c * step, step)],
            send_sem=part_send.at[CHUNKS * layer + c],
            recv_sem=part_recv.at[CHUNKS * layer + c],
            device_id={"chan": other},
            device_id_type=MESH,
        )

    def diff_copy(c):
        return pltpu.make_async_remote_copy(
            src_ref=diff_sent.at[pl.ds(c * half, half)],
            dst_ref=diff_got.at[pl.ds(c * half, half)],
            send_sem=diff_send.at[c],
            recv_sem=diff_recv.at[c],
            device_id={"chan": other},
            device_id_type=MESH,
        )

    places = bases.shape[1]
    columns = 4 * places
    spread = (
        lax.broadcasted_iota(jnp.int32, (places, columns), 1) // 4
        == lax.broadcasted_iota(jnp.int32, (places, columns), 0)
    ).astype(F32).astype(BF16)
    code = (lax.broadcasted_iota(jnp.int32, (1, columns), 1) % 4).astype(F32)

    def activate(layer, value):
        return gelu(
            value.astype(F32) * scale[layer : layer + 1, :] + shift[layer : layer + 1, :]
        ).astype(BF16)

    def start(c):
        at = pl.ds(c * step, step)
        repeated = dot(bases[at].astype(F32).astype(BF16), spread)
        onehot = jnp.where(repeated == code, 1.0, 0.0).astype(BF16)
        value = (tower[at].astype(F32) + dot(onehot, embed[...])).astype(BF16)
        stream[at] = value
        padded0[pl.ds(PAD + c * step, step)] = activate(0, value)

    def convolve(layer, c):
        d = SPACINGS[layer]
        base = PAD + c * step
        taps = jnp.concatenate(
            [padded[layer][pl.ds(base + k * d, step)] for k in (-1, 0, 1)], axis=1
        )
        sent[layer, pl.ds(c * step, step)] = dot(taps, conv[layer]).astype(BF16)
        part_copy(layer, c).start()

    def pairs(c):
        return tuple(
            jnp.concatenate(
                [final[j, pl.ds(c * step + r, half, stride=2)] for j in range(width // LANES)], axis=1
            )
            for r in range(2)
        )

    def finish(layer, c):
        at = pl.ds(c * step, step)
        part_copy(layer, c).wait_recv()
        total = sent[layer, at].astype(F32) + got[layer, at].astype(F32)
        gain = jnp.concatenate([mids[0, 0, layer : layer + 1], mids[1, 0, layer : layer + 1]], axis=1)
        bias = jnp.concatenate([mids[0, 1, layer : layer + 1], mids[1, 1, layer : layer + 1]], axis=1)
        inner = gelu(total * gain + bias).astype(BF16)
        value = stream[at].astype(F32) + dot(inner, point[layer])
        if layer == 0:
            value = value.astype(BF16)
            stream[at] = value
            padded1[pl.ds(PAD + c * step, step)] = activate(1, value)
        else:
            for j in range(width // LANES):
                final[j, at] = value[:, j * LANES : (j + 1) * LANES]
            even, odd = pairs(c)
            diff_sent[pl.ds(c * half, half)] = (even - odd).astype(BF16)
            diff_copy(c).start()

    def emit(c):
        at = pl.ds(c * half, half)
        logits = dot(diff_sent[at], pool[0])
        diff_copy(c).wait_recv()
        logits = logits + dot(diff_got[at], pool[1])
        weigh = 0.5 + 0.5 * jnp.tanh(0.5 * logits)
        even, odd = pairs(c)
        result[at] = (odd + weigh * (even - odd)).astype(BF16)
        pltpu.make_async_copy(result.at[at], out_h.at[at], out_sem.at[c]).start()

    for name in ("bases", "embed", "tower", "scale", "shift"):
        loads[name].wait()
    last = CHUNKS - 1
    start(0)
    start(last)
    pl.semaphore_wait(
        barrier,
        1 + jnp.where(seq > 0, 1, 0) + jnp.where(seq < seq_count - 1, 1, 0),
    )
    send_left(0)
    send_right(0)
    for which in range(2):
        loads["mid%d" % which].wait()
        mid_copy(which).start()
    for c in range(1, last):
        start(c)

    for tap in range(3):
        loads[("conv", 0, tap)].wait()
    convolve(0, 1)
    convolve(0, 2)
    loads[("point", 0)].wait()
    for which in range(2):
        mid_copy(which).wait_recv()
    finish(0, 1)
    wait_left_rim(0)
    convolve(0, 0)
    finish(0, 2)
    wait_right_rim(0)
    convolve(0, 3)
    finish(0, 0)
    send_left(1)
    for tap in range(3):
        loads[("conv", 1, tap)].wait()
    convolve(1, 1)
    finish(0, 3)
    send_right(1)
    convolve(1, 2)
    loads[("point", 1)].wait()
    finish(1, 1)
    wait_left_rim(1)
    convolve(1, 0)
    finish(1, 2)
    wait_right_rim(1)
    convolve(1, 3)
    loads["pool0"].wait()
    loads["pool1"].wait()
    finish(1, 0)
    emit(1)
    finish(1, 3)
    emit(2)
    emit(0)
    emit(3)

    for layer in range(2):
        @pl.when(seq < seq_count - 1)
        def _():
            to_right(layer).wait_send()

        @pl.when(seq > 0)
        def _():
            to_left(layer).wait_send()

        mid_copy(layer).wait_send()
        for c in range(CHUNKS):
            part_copy(layer, c).wait_send()
    for c in range(CHUNKS):
        diff_copy(c).wait_send()
        at = pl.ds(c * half, half)
        pltpu.make_async_copy(result.at[at], out_h.at[at], out_sem.at[c]).wait()


def local(seq_count, tower_input, dna_bases, base_embed, in_scale, entry_norm_shift, conv_w, mid_scale, mid_shift, point_w, pooling_weight):
    rows, width = tower_input.shape
    inner = point_w.shape[1]
    anywhere = pl.BlockSpec(memory_space=pl.ANY)
    dma = pltpu.SemaphoreType.DMA
    return pl.pallas_call(
        functools.partial(kernel, seq_count),
        out_shape=jax.ShapeDtypeStruct((rows // 2, width), BF16),
        in_specs=[anywhere] * 10,
        out_specs=anywhere,
        scratch_shapes=[
            pltpu.VMEM((rows, width), BF16),
            pltpu.VMEM(dna_bases.shape, jnp.int32),
            pltpu.VMEM(base_embed.shape, BF16),
            pltpu.VMEM(in_scale.shape, F32),
            pltpu.VMEM(entry_norm_shift.shape, F32),
            pltpu.VMEM((2, 3 * width, inner), BF16),
            pltpu.VMEM((2, 2) + mid_scale.shape, F32),
            pltpu.VMEM(point_w.shape, BF16),
            pltpu.VMEM((2, width, width), BF16),
            pltpu.VMEM((rows, width), BF16),
            pltpu.VMEM((rows + 2 * PAD, width), BF16),
            pltpu.VMEM((rows + 2 * PAD, width), BF16),
            pltpu.VMEM((2, rows, inner), BF16),
            pltpu.VMEM((2, rows, inner), BF16),
            pltpu.VMEM((width // LANES, rows, LANES), F32),
            pltpu.VMEM((rows // 2, width), BF16),
            pltpu.VMEM((rows // 2, width), BF16),
            pltpu.VMEM((rows // 2, width), BF16),
            dma((11,)),
            dma((6,)),
            dma((4,)),
            dma((4,)),
            dma((4,)),
            dma((2 * CHUNKS,)),
            dma((2 * CHUNKS,)),
            dma((CHUNKS,)),
            dma((CHUNKS,)),
            dma((CHUNKS,)),
        ],
        compiler_params=pltpu.CompilerParams(
            collective_id=0, has_side_effects=True, vmem_limit_bytes=56 * 1024 * 1024
        ),
    )(tower_input, dna_bases, base_embed, in_scale, entry_norm_shift, conv_w, mid_scale, mid_shift, point_w, pooling_weight)


def solution(mesh):
    return jax.shard_map(
        functools.partial(local, mesh.shape["seq"]),
        mesh=mesh,
        in_specs=(
            P(("groups", "seq"), "chan"),
            P(("groups", "seq"), None),
            P(None, "chan"),
            P(None, "chan"),
            P(None, "chan"),
            P(None, None, "chan", None),
            P(None, "chan"),
            P(None, "chan"),
            P(None, None, "chan"),
            P(None, "chan"),
        ),
        out_specs=P(("groups", "seq"), "chan"),
        check_vma=False,
    )
```

```python
import functools

import jax
import jax.numpy as jnp
from jax import lax
from jax.experimental import pallas as pl
from jax.experimental.pallas import tpu as pltpu
from jax.sharding import PartitionSpec as P

SPACINGS = (32, 48)
PAD = 48
CHUNKS = 4
LANES = 128
MESH = pl.DeviceIdType.MESH
F32 = jnp.float32
BF16 = jnp.bfloat16
GELU_A = 0.7978845608028654
GELU_B = 0.7978845608028654 * 0.044715


def gelu(v):
    half = 0.5 * v
    return half + half * jnp.tanh(v * (GELU_A + GELU_B * (v * v)))


def dot(a, b):
    return jnp.dot(a, b, preferred_element_type=F32)


def kernel(
    seq_count,
    tower_h,
    bases_h,
    embed_h,
    scale_h,
    shift_h,
    conv_h,
    mid_scale_h,
    mid_shift_h,
    point_h,
    pool_h,
    out,
    tower,
    bases,
    embed,
    scale,
    shift,
    conv,
    mids,
    point,
    pool,
    stream,
    padded0,
    padded1,
    sent,
    got,
    final,
    diff_sent,
    diff_got,
    load_sem,
    conv_sem,
    mid_sem,
    halo_send,
    halo_recv,
    part_send,
    part_recv,
    diff_send,
    diff_recv,
):
    seq = lax.axis_index("seq")
    me = lax.axis_index("chan")
    other = 1 - me
    rows, width = tower.shape
    step = rows // CHUNKS
    half = step // 2
    padded = (padded0, padded1)

    loads = {}

    def load(name, src, dst, sem):
        copy = pltpu.make_async_copy(src, dst, sem)
        copy.start()
        loads[name] = copy

    load("bases", bases_h, bases, load_sem.at[0])
    load("embed", embed_h, embed, load_sem.at[1])
    load("tower", tower_h, tower, load_sem.at[2])
    load("scale", scale_h, scale, load_sem.at[3])
    load("shift", shift_h, shift, load_sem.at[4])
    load("mid0", mid_scale_h, mids.at[me, 0], load_sem.at[5])
    load("mid1", mid_shift_h, mids.at[me, 1], load_sem.at[6])
    for layer in range(2):
        for tap in range(3):
            load(
                ("conv", layer, tap),
                conv_h.at[layer, tap],
                conv.at[layer, pl.ds(tap * width, width)],
                conv_sem.at[3 * layer + tap],
            )
        load(("point", layer), point_h.at[layer], point.at[layer], load_sem.at[7 + layer])
    load("pool0", pool_h.at[pl.ds(pl.multiple_of(me * width, width), width)], pool.at[0], load_sem.at[9])
    load("pool1", pool_h.at[pl.ds(pl.multiple_of(other * width, width), width)], pool.at[1], load_sem.at[10])

    edge = jnp.zeros((PAD, width), BF16)
    for buffer in padded:
        buffer[0:PAD] = edge
        buffer[PAD + rows : PAD + rows + PAD] = edge

    barrier = pltpu.get_barrier_semaphore()
    pl.semaphore_signal(barrier, inc=1, device_id={"chan": other}, device_id_type=MESH)

    @pl.when(seq > 0)
    def _():
        pl.semaphore_signal(barrier, inc=1, device_id={"seq": seq - 1}, device_id_type=MESH)

    @pl.when(seq < seq_count - 1)
    def _():
        pl.semaphore_signal(barrier, inc=1, device_id={"seq": seq + 1}, device_id_type=MESH)

    def to_right(layer):
        d = SPACINGS[layer]
        return pltpu.make_async_remote_copy(
            src_ref=padded[layer].at[pl.ds(PAD + rows - d, d)],
            dst_ref=padded[layer].at[pl.ds(PAD - d, d)],
            send_sem=halo_send.at[2 * layer],
            recv_sem=halo_recv.at[2 * layer],
            device_id={"seq": seq + 1},
            device_id_type=MESH,
        )

    def to_left(layer):
        d = SPACINGS[layer]
        return pltpu.make_async_remote_copy(
            src_ref=padded[layer].at[pl.ds(PAD, d)],
            dst_ref=padded[layer].at[pl.ds(PAD + rows, d)],
            send_sem=halo_send.at[2 * layer + 1],
            recv_sem=halo_recv.at[2 * layer + 1],
            device_id={"seq": seq - 1},
            device_id_type=MESH,
        )

    def send_right(layer):
        @pl.when(seq < seq_count - 1)
        def _():
            to_right(layer).start()

    def send_left(layer):
        @pl.when(seq > 0)
        def _():
            to_left(layer).start()

    def wait_left_rim(layer):
        @pl.when(seq > 0)
        def _():
            to_right(layer).wait_recv()

    def wait_right_rim(layer):
        @pl.when(seq < seq_count - 1)
        def _():
            to_left(layer).wait_recv()

    def mid_copy(which):
        return pltpu.make_async_remote_copy(
            src_ref=mids.at[me, which],
            dst_ref=mids.at[me, which],
            send_sem=mid_sem.at[which],
            recv_sem=mid_sem.at[2 + which],
            device_id={"chan": other},
            device_id_type=MESH,
        )

    def part_copy(layer, c):
        return pltpu.make_async_remote_copy(
            src_ref=sent.at[layer, pl.ds(c * step, step)],
            dst_ref=got.at[layer, pl.ds(c * step, step)],
            send_sem=part_send.at[CHUNKS * layer + c],
            recv_sem=part_recv.at[CHUNKS * layer + c],
            device_id={"chan": other},
            device_id_type=MESH,
        )

    def diff_copy(c):
        return pltpu.make_async_remote_copy(
            src_ref=diff_sent.at[pl.ds(c * half, half)],
            dst_ref=diff_got.at[pl.ds(c * half, half)],
            send_sem=diff_send.at[c],
            recv_sem=diff_recv.at[c],
            device_id={"chan": other},
            device_id_type=MESH,
        )

    places = bases.shape[0]
    columns = 4 * places
    spread = (
        lax.broadcasted_iota(jnp.int32, (places, columns), 1) // 4
        == lax.broadcasted_iota(jnp.int32, (places, columns), 0)
    ).astype(F32).astype(BF16)
    code = (lax.broadcasted_iota(jnp.int32, (1, columns), 1) % 4).astype(F32)

    def activate(layer, value):
        return gelu(
            value.astype(F32) * scale[layer : layer + 1, :] + shift[layer : layer + 1, :]
        ).astype(BF16)

    def start(c):
        at = pl.ds(c * step, step)
        repeated = lax.dot_general(
            bases[:, at].astype(F32).astype(BF16),
            spread,
            (((0,), (0,)), ((), ())),
            preferred_element_type=F32,
        )
        onehot = jnp.where(repeated == code, 1.0, 0.0).astype(BF16)
        value = (tower[at].astype(F32) + dot(onehot, embed[...])).astype(BF16)
        stream[at] = value
        padded0[pl.ds(PAD + c * step, step)] = activate(0, value)

    def convolve(layer, c):
        d = SPACINGS[layer]
        base = PAD + c * step
        taps = jnp.concatenate(
            [padded[layer][pl.ds(base + k * d, step)] for k in (-1, 0, 1)], axis=1
        )
        sent[layer, pl.ds(c * step, step)] = dot(taps, conv[layer]).astype(BF16)
        part_copy(layer, c).start()

    def pairs(c):
        return tuple(
            jnp.concatenate(
                [final[j, pl.ds(c * step + r, half, stride=2)] for j in range(width // LANES)], axis=1
            )
            for r in range(2)
        )

    def finish(layer, c):
        at = pl.ds(c * step, step)
        part_copy(layer, c).wait_recv()
        total = sent[layer, at].astype(F32) + got[layer, at].astype(F32)
        gain = jnp.concatenate([mids[0, 0, layer : layer + 1], mids[1, 0, layer : layer + 1]], axis=1)
        bias = jnp.concatenate([mids[0, 1, layer : layer + 1], mids[1, 1, layer : layer + 1]], axis=1)
        inner = gelu(total * gain + bias).astype(BF16)
        value = stream[at].astype(F32) + dot(inner, point[layer])
        if layer == 0:
            value = value.astype(BF16)
            stream[at] = value
            padded1[pl.ds(PAD + c * step, step)] = activate(1, value)
        else:
            for j in range(width // LANES):
                final[j, at] = value[:, j * LANES : (j + 1) * LANES]
            even, odd = pairs(c)
            diff_sent[pl.ds(c * half, half)] = (even - odd).astype(BF16)
            diff_copy(c).start()

    def emit(c):
        at = pl.ds(c * half, half)
        logits = dot(diff_sent[at], pool[0])
        diff_copy(c).wait_recv()
        logits = logits + dot(diff_got[at], pool[1])
        weigh = 0.5 + 0.5 * jnp.tanh(0.5 * logits)
        even, odd = pairs(c)
        out[at] = (odd + weigh * (even - odd)).astype(BF16)

    for name in ("bases", "embed", "tower", "scale", "shift"):
        loads[name].wait()
    last = CHUNKS - 1
    start(0)
    start(last)
    pl.semaphore_wait(
        barrier,
        1 + jnp.where(seq > 0, 1, 0) + jnp.where(seq < seq_count - 1, 1, 0),
    )
    send_left(0)
    send_right(0)
    for which in range(2):
        loads["mid%d" % which].wait()
        mid_copy(which).start()
    for c in range(1, last):
        start(c)

    for tap in range(3):
        loads[("conv", 0, tap)].wait()
    convolve(0, 1)
    convolve(0, 2)
    loads[("point", 0)].wait()
    for which in range(2):
        mid_copy(which).wait_recv()
    finish(0, 1)
    wait_left_rim(0)
    convolve(0, 0)
    finish(0, 2)
    wait_right_rim(0)
    convolve(0, 3)
    finish(0, 0)
    send_left(1)
    for tap in range(3):
        loads[("conv", 1, tap)].wait()
    convolve(1, 1)
    finish(0, 3)
    send_right(1)
    convolve(1, 2)
    loads[("point", 1)].wait()
    finish(1, 1)
    wait_left_rim(1)
    convolve(1, 0)
    finish(1, 2)
    wait_right_rim(1)
    convolve(1, 3)
    loads["pool0"].wait()
    loads["pool1"].wait()
    finish(1, 0)
    emit(1)
    finish(1, 3)
    emit(2)
    emit(0)
    emit(3)

    for layer in range(2):
        @pl.when(seq < seq_count - 1)
        def _():
            to_right(layer).wait_send()

        @pl.when(seq > 0)
        def _():
            to_left(layer).wait_send()

        mid_copy(layer).wait_send()
        for c in range(CHUNKS):
            part_copy(layer, c).wait_send()
    for c in range(CHUNKS):
        diff_copy(c).wait_send()


def local(seq_count, tower_input, dna_bases, base_embed, in_scale, entry_norm_shift, conv_w, mid_scale, mid_shift, point_w, pooling_weight):
    rows, width = tower_input.shape
    inner = point_w.shape[1]
    anywhere = pl.BlockSpec(memory_space=pl.ANY)
    dma = pltpu.SemaphoreType.DMA
    return pl.pallas_call(
        functools.partial(kernel, seq_count),
        out_shape=pltpu.VMEM((rows // 2, width), BF16),
        in_specs=[anywhere] * 10,
        out_specs=pl.BlockSpec(memory_space=pltpu.VMEM),
        scratch_shapes=[
            pltpu.VMEM((rows, width), BF16),
            pltpu.VMEM(dna_bases.shape[::-1], jnp.int32),
            pltpu.VMEM(base_embed.shape, BF16),
            pltpu.VMEM(in_scale.shape, F32),
            pltpu.VMEM(entry_norm_shift.shape, F32),
            pltpu.VMEM((2, 3 * width, inner), BF16),
            pltpu.VMEM((2, 2) + mid_scale.shape, F32),
            pltpu.VMEM(point_w.shape, BF16),
            pltpu.VMEM((2, width, width), BF16),
            pltpu.VMEM((rows, width), BF16),
            pltpu.VMEM((rows + 2 * PAD, width), BF16),
            pltpu.VMEM((rows + 2 * PAD, width), BF16),
            pltpu.VMEM((2, rows, inner), BF16),
            pltpu.VMEM((2, rows, inner), BF16),
            pltpu.VMEM((width // LANES, rows, LANES), F32),
            pltpu.VMEM((rows // 2, width), BF16),
            pltpu.VMEM((rows // 2, width), BF16),
            dma((11,)),
            dma((6,)),
            dma((4,)),
            dma((4,)),
            dma((4,)),
            dma((2 * CHUNKS,)),
            dma((2 * CHUNKS,)),
            dma((CHUNKS,)),
            dma((CHUNKS,)),
        ],
        compiler_params=pltpu.CompilerParams(
            collective_id=0, has_side_effects=True, vmem_limit_bytes=56 * 1024 * 1024
        ),
    )(tower_input, dna_bases.T, base_embed, in_scale, entry_norm_shift, conv_w, mid_scale, mid_shift, point_w, pooling_weight)


def solution(mesh):
    return jax.shard_map(
        functools.partial(local, mesh.shape["seq"]),
        mesh=mesh,
        in_specs=(
            P(("groups", "seq"), "chan"),
            P(("groups", "seq"), None),
            P(None, "chan"),
            P(None, "chan"),
            P(None, "chan"),
            P(None, None, "chan", None),
            P(None, "chan"),
            P(None, "chan"),
            P(None, None, "chan"),
            P(None, "chan"),
        ),
        out_specs=P(("groups", "seq"), "chan"),
        check_vma=False,
    )
```

```python
import functools

import jax
import jax.numpy as jnp
from jax import lax
from jax.experimental import pallas as pl
from jax.experimental.pallas import tpu as pltpu
from jax.sharding import PartitionSpec as P

SPACINGS = (32, 48)
PAD = 48
CHUNKS = 4
LANES = 128
MESH = pl.DeviceIdType.MESH
F32 = jnp.float32
BF16 = jnp.bfloat16
GELU_A = 0.7978845608028654
GELU_B = 0.7978845608028654 * 0.044715


def gelu(v):
    half = 0.5 * v
    return half + half * jnp.tanh(v * (GELU_A + GELU_B * (v * v)))


def dot(a, b):
    return jnp.dot(a, b, preferred_element_type=F32)


def kernel(
    seq_count,
    tower_h,
    bases_h,
    embed_h,
    scale_h,
    shift_h,
    conv_h,
    mid_scale_h,
    mid_shift_h,
    point_h,
    pool_h,
    out,
    tower,
    bases,
    embed,
    scale,
    shift,
    conv,
    mids,
    point,
    pool,
    stream,
    padded0,
    padded1,
    sent,
    got,
    final,
    diff_sent,
    diff_got,
    load_sem,
    conv_sem,
    mid_sem,
    halo_send,
    halo_recv,
    part_send,
    part_recv,
    diff_send,
    diff_recv,
):
    seq = lax.axis_index("seq")
    me = lax.axis_index("chan")
    other = 1 - me
    rows, width = tower.shape
    step = rows // CHUNKS
    half = step // 2
    padded = (padded0, padded1)

    loads = {}

    def load(name, src, dst, sem):
        copy = pltpu.make_async_copy(src, dst, sem)
        copy.start()
        loads[name] = copy

    load("bases", bases_h, bases, load_sem.at[0])
    load("embed", embed_h, embed, load_sem.at[1])
    load("tower", tower_h, tower, load_sem.at[2])
    load("scale", scale_h, scale, load_sem.at[3])
    load("shift", shift_h, shift, load_sem.at[4])
    load("mid0", mid_scale_h, mids.at[me, 0], load_sem.at[5])
    load("mid1", mid_shift_h, mids.at[me, 1], load_sem.at[6])
    def load_block(layer):
        for tap in range(3):
            load(
                ("conv", layer, tap),
                conv_h.at[layer, tap],
                conv.at[layer, pl.ds(tap * width, width)],
                conv_sem.at[3 * layer + tap],
            )
        load(("point", layer), point_h.at[layer], point.at[layer], load_sem.at[7 + layer])

    edge = jnp.zeros((PAD, width), BF16)
    for buffer in padded:
        buffer[0:PAD] = edge
        buffer[PAD + rows : PAD + rows + PAD] = edge

    barrier = pltpu.get_barrier_semaphore()
    pl.semaphore_signal(barrier, inc=1, device_id={"chan": other}, device_id_type=MESH)

    @pl.when(seq > 0)
    def _():
        pl.semaphore_signal(barrier, inc=1, device_id={"seq": seq - 1}, device_id_type=MESH)

    @pl.when(seq < seq_count - 1)
    def _():
        pl.semaphore_signal(barrier, inc=1, device_id={"seq": seq + 1}, device_id_type=MESH)

    def to_right(layer):
        d = SPACINGS[layer]
        return pltpu.make_async_remote_copy(
            src_ref=padded[layer].at[pl.ds(PAD + rows - d, d)],
            dst_ref=padded[layer].at[pl.ds(PAD - d, d)],
            send_sem=halo_send.at[2 * layer],
            recv_sem=halo_recv.at[2 * layer],
            device_id={"seq": seq + 1},
            device_id_type=MESH,
        )

    def to_left(layer):
        d = SPACINGS[layer]
        return pltpu.make_async_remote_copy(
            src_ref=padded[layer].at[pl.ds(PAD, d)],
            dst_ref=padded[layer].at[pl.ds(PAD + rows, d)],
            send_sem=halo_send.at[2 * layer + 1],
            recv_sem=halo_recv.at[2 * layer + 1],
            device_id={"seq": seq - 1},
            device_id_type=MESH,
        )

    def send_right(layer):
        @pl.when(seq < seq_count - 1)
        def _():
            to_right(layer).start()

    def send_left(layer):
        @pl.when(seq > 0)
        def _():
            to_left(layer).start()

    def wait_left_rim(layer):
        @pl.when(seq > 0)
        def _():
            to_right(layer).wait_recv()

    def wait_right_rim(layer):
        @pl.when(seq < seq_count - 1)
        def _():
            to_left(layer).wait_recv()

    def mid_copy(which):
        return pltpu.make_async_remote_copy(
            src_ref=mids.at[me, which],
            dst_ref=mids.at[me, which],
            send_sem=mid_sem.at[which],
            recv_sem=mid_sem.at[2 + which],
            device_id={"chan": other},
            device_id_type=MESH,
        )

    def part_copy(layer, c):
        return pltpu.make_async_remote_copy(
            src_ref=sent.at[layer, pl.ds(c * step, step)],
            dst_ref=got.at[layer, pl.ds(c * step, step)],
            send_sem=part_send.at[CHUNKS * layer + c],
            recv_sem=part_recv.at[CHUNKS * layer + c],
            device_id={"chan": other},
            device_id_type=MESH,
        )

    def diff_copy(c):
        return pltpu.make_async_remote_copy(
            src_ref=diff_sent.at[pl.ds(c * half, half)],
            dst_ref=diff_got.at[pl.ds(c * half, half)],
            send_sem=diff_send.at[c],
            recv_sem=diff_recv.at[c],
            device_id={"chan": other},
            device_id_type=MESH,
        )

    places = bases.shape[0]
    columns = 4 * places
    spread = (
        lax.broadcasted_iota(jnp.int32, (places, columns), 1) // 4
        == lax.broadcasted_iota(jnp.int32, (places, columns), 0)
    ).astype(F32).astype(BF16)
    code = (lax.broadcasted_iota(jnp.int32, (1, columns), 1) % 4).astype(F32)

    def activate(layer, value):
        return gelu(
            value.astype(F32) * scale[layer : layer + 1, :] + shift[layer : layer + 1, :]
        ).astype(BF16)

    def start(c):
        at = pl.ds(c * step, step)
        repeated = lax.dot_general(
            bases[:, at].astype(F32).astype(BF16),
            spread,
            (((0,), (0,)), ((), ())),
            preferred_element_type=F32,
        )
        onehot = jnp.where(repeated == code, 1.0, 0.0).astype(BF16)
        value = (tower[at].astype(F32) + dot(onehot, embed[...])).astype(BF16)
        stream[at] = value
        padded0[pl.ds(PAD + c * step, step)] = activate(0, value)

    def convolve(layer, c):
        d = SPACINGS[layer]
        base = PAD + c * step
        taps = jnp.concatenate(
            [padded[layer][pl.ds(base + k * d, step)] for k in (-1, 0, 1)], axis=1
        )
        sent[layer, pl.ds(c * step, step)] = dot(taps, conv[layer]).astype(BF16)

    def pairs(c):
        return tuple(
            jnp.concatenate(
                [final[j, pl.ds(c * step + r, half, stride=2)] for j in range(width // LANES)], axis=1
            )
            for r in range(2)
        )

    def finish(layer, c):
        at = pl.ds(c * step, step)
        total = sent[layer, at].astype(F32) + got[layer, at].astype(F32)
        gain = jnp.concatenate([mids[0, 0, layer : layer + 1], mids[1, 0, layer : layer + 1]], axis=1)
        bias = jnp.concatenate([mids[0, 1, layer : layer + 1], mids[1, 1, layer : layer + 1]], axis=1)
        inner = gelu(total * gain + bias).astype(BF16)
        value = stream[at].astype(F32) + dot(inner, point[layer])
        if layer == 0:
            value = value.astype(BF16)
            stream[at] = value
            padded1[pl.ds(PAD + c * step, step)] = activate(1, value)
        else:
            for j in range(width // LANES):
                final[j, at] = value[:, j * LANES : (j + 1) * LANES]
            even, odd = pairs(c)
            diff_sent[pl.ds(c * half, half)] = (even - odd).astype(BF16)

    def emit(c):
        at = pl.ds(c * half, half)
        logits = dot(diff_sent[at], pool[0])
        logits = logits + dot(diff_got[at], pool[1])
        weigh = 0.5 + 0.5 * jnp.tanh(0.5 * logits)
        even, odd = pairs(c)
        out[at] = (odd + weigh * (even - odd)).astype(BF16)

    def together(conv_at=None, finish_at=None, emit_at=None):
        if finish_at is not None:
            part_copy(*finish_at).wait_recv()
        if emit_at is not None:
            diff_copy(emit_at).wait_recv()
        if conv_at is not None:
            convolve(*conv_at)
        if emit_at is not None:
            emit(emit_at)
        if finish_at is not None:
            finish(*finish_at)
        if conv_at is not None:
            part_copy(*conv_at).start()
        if finish_at is not None and finish_at[0] == 1:
            diff_copy(finish_at[1]).start()

    for name in ("bases", "embed", "tower", "scale", "shift"):
        loads[name].wait()
    load_block(0)
    last = CHUNKS - 1
    start(0)
    start(last)
    pl.semaphore_wait(
        barrier,
        1 + jnp.where(seq > 0, 1, 0) + jnp.where(seq < seq_count - 1, 1, 0),
    )
    send_left(0)
    send_right(0)
    for which in range(2):
        loads["mid%d" % which].wait()
        mid_copy(which).start()
    for c in range(1, last):
        start(c)

    for tap in range(3):
        loads[("conv", 0, tap)].wait()
    load_block(1)
    load("pool0", pool_h.at[pl.ds(pl.multiple_of(me * width, width), width)], pool.at[0], load_sem.at[9])
    load("pool1", pool_h.at[pl.ds(pl.multiple_of(other * width, width), width)], pool.at[1], load_sem.at[10])
    together(conv_at=(0, 1))
    together(conv_at=(0, 2))
    loads[("point", 0)].wait()
    for which in range(2):
        mid_copy(which).wait_recv()
    wait_left_rim(0)
    together(conv_at=(0, 0), finish_at=(0, 1))
    wait_right_rim(0)
    together(conv_at=(0, 3), finish_at=(0, 2))
    together(finish_at=(0, 0))
    send_left(1)
    for tap in range(3):
        loads[("conv", 1, tap)].wait()
    together(conv_at=(1, 1), finish_at=(0, 3))
    send_right(1)
    together(conv_at=(1, 2))
    loads[("point", 1)].wait()
    wait_right_rim(1)
    together(conv_at=(1, 3), finish_at=(1, 1))
    loads["pool0"].wait()
    loads["pool1"].wait()
    wait_left_rim(1)
    together(conv_at=(1, 0), finish_at=(1, 2))
    together(finish_at=(1, 3), emit_at=1)
    together(finish_at=(1, 0), emit_at=2)
    together(emit_at=3)
    together(emit_at=0)

    for layer in range(2):
        @pl.when(seq < seq_count - 1)
        def _():
            to_right(layer).wait_send()

        @pl.when(seq > 0)
        def _():
            to_left(layer).wait_send()

        mid_copy(layer).wait_send()
        for c in range(CHUNKS):
            part_copy(layer, c).wait_send()
    for c in range(CHUNKS):
        diff_copy(c).wait_send()


def local(seq_count, tower_input, dna_bases, base_embed, in_scale, entry_norm_shift, conv_w, mid_scale, mid_shift, point_w, pooling_weight):
    rows, width = tower_input.shape
    inner = point_w.shape[1]
    anywhere = pl.BlockSpec(memory_space=pl.ANY)
    dma = pltpu.SemaphoreType.DMA
    return pl.pallas_call(
        functools.partial(kernel, seq_count),
        out_shape=pltpu.VMEM((rows // 2, width), BF16),
        in_specs=[anywhere] * 10,
        out_specs=pl.BlockSpec(memory_space=pltpu.VMEM),
        scratch_shapes=[
            pltpu.VMEM((rows, width), BF16),
            pltpu.VMEM(dna_bases.shape[::-1], jnp.int32),
            pltpu.VMEM(base_embed.shape, BF16),
            pltpu.VMEM(in_scale.shape, F32),
            pltpu.VMEM(entry_norm_shift.shape, F32),
            pltpu.VMEM((2, 3 * width, inner), BF16),
            pltpu.VMEM((2, 2) + mid_scale.shape, F32),
            pltpu.VMEM(point_w.shape, BF16),
            pltpu.VMEM((2, width, width), BF16),
            pltpu.VMEM((rows, width), BF16),
            pltpu.VMEM((rows + 2 * PAD, width), BF16),
            pltpu.VMEM((rows + 2 * PAD, width), BF16),
            pltpu.VMEM((2, rows, inner), BF16),
            pltpu.VMEM((2, rows, inner), BF16),
            pltpu.VMEM((width // LANES, rows, LANES), F32),
            pltpu.VMEM((rows // 2, width), BF16),
            pltpu.VMEM((rows // 2, width), BF16),
            dma((11,)),
            dma((6,)),
            dma((4,)),
            dma((4,)),
            dma((4,)),
            dma((2 * CHUNKS,)),
            dma((2 * CHUNKS,)),
            dma((CHUNKS,)),
            dma((CHUNKS,)),
        ],
        compiler_params=pltpu.CompilerParams(
            collective_id=0, has_side_effects=True, vmem_limit_bytes=56 * 1024 * 1024
        ),
    )(tower_input, dna_bases.T, base_embed, in_scale, entry_norm_shift, conv_w, mid_scale, mid_shift, point_w, pooling_weight)


def solution(mesh):
    return jax.shard_map(
        functools.partial(local, mesh.shape["seq"]),
        mesh=mesh,
        in_specs=(
            P(("groups", "seq"), "chan"),
            P(("groups", "seq"), None),
            P(None, "chan"),
            P(None, "chan"),
            P(None, "chan"),
            P(None, None, "chan", None),
            P(None, "chan"),
            P(None, "chan"),
            P(None, None, "chan"),
            P(None, "chan"),
        ),
        out_specs=P(("groups", "seq"), "chan"),
        check_vma=False,
    )
```

```python
import functools

import jax
import jax.numpy as jnp
from jax import lax
from jax.experimental import pallas as pl
from jax.experimental.pallas import tpu as pltpu
from jax.sharding import PartitionSpec as P

SPACINGS = (32, 48)
PAD = 48
CHUNKS = 4
LANES = 128
MESH = pl.DeviceIdType.MESH
F32 = jnp.float32
BF16 = jnp.bfloat16
GELU_A = 0.7978845608028654
GELU_B = 0.7978845608028654 * 0.044715


def gelu(v):
    half = (0.5 * v).astype(BF16)
    bent = jnp.tanh((v * (GELU_A + GELU_B * (v * v))).astype(BF16))
    return half + half * bent


def dot(a, b):
    return jnp.dot(a, b, preferred_element_type=F32)


def kernel(
    seq_count,
    tower_h,
    bases_h,
    embed_h,
    scale_h,
    shift_h,
    conv_h,
    mid_scale_h,
    mid_shift_h,
    point_h,
    pool_h,
    out,
    tower,
    bases,
    embed,
    scale,
    shift,
    conv,
    mids,
    point,
    pool,
    stream,
    padded0,
    padded1,
    sent,
    got,
    final,
    diff_sent,
    diff_got,
    load_sem,
    conv_sem,
    mid_sem,
    halo_send,
    halo_recv,
    part_send,
    part_recv,
    diff_send,
    diff_recv,
):
    seq = lax.axis_index("seq")
    me = lax.axis_index("chan")
    other = 1 - me
    rows, width = tower.shape
    step = rows // CHUNKS
    half = step // 2
    padded = (padded0, padded1)

    loads = {}

    def load(name, src, dst, sem):
        copy = pltpu.make_async_copy(src, dst, sem)
        copy.start()
        loads[name] = copy

    load("bases", bases_h, bases, load_sem.at[0])
    load("embed", embed_h, embed, load_sem.at[1])
    load("tower", tower_h, tower, load_sem.at[2])
    load("scale", scale_h, scale, load_sem.at[3])
    load("shift", shift_h, shift, load_sem.at[4])
    load("mid0", mid_scale_h, mids.at[me, 0], load_sem.at[5])
    load("mid1", mid_shift_h, mids.at[me, 1], load_sem.at[6])
    def load_block(layer):
        for tap in range(3):
            load(
                ("conv", layer, tap),
                conv_h.at[layer, tap],
                conv.at[layer, pl.ds(tap * width, width)],
                conv_sem.at[3 * layer + tap],
            )
        load(("point", layer), point_h.at[layer], point.at[layer], load_sem.at[7 + layer])

    edge = jnp.zeros((PAD, width), BF16)
    for buffer in padded:
        buffer[0:PAD] = edge
        buffer[PAD + rows : PAD + rows + PAD] = edge

    barrier = pltpu.get_barrier_semaphore()
    pl.semaphore_signal(barrier, inc=1, device_id={"chan": other}, device_id_type=MESH)

    @pl.when(seq > 0)
    def _():
        pl.semaphore_signal(barrier, inc=1, device_id={"seq": seq - 1}, device_id_type=MESH)

    @pl.when(seq < seq_count - 1)
    def _():
        pl.semaphore_signal(barrier, inc=1, device_id={"seq": seq + 1}, device_id_type=MESH)

    def to_right(layer):
        d = SPACINGS[layer]
        return pltpu.make_async_remote_copy(
            src_ref=padded[layer].at[pl.ds(PAD + rows - d, d)],
            dst_ref=padded[layer].at[pl.ds(PAD - d, d)],
            send_sem=halo_send.at[2 * layer],
            recv_sem=halo_recv.at[2 * layer],
            device_id={"seq": seq + 1},
            device_id_type=MESH,
        )

    def to_left(layer):
        d = SPACINGS[layer]
        return pltpu.make_async_remote_copy(
            src_ref=padded[layer].at[pl.ds(PAD, d)],
            dst_ref=padded[layer].at[pl.ds(PAD + rows, d)],
            send_sem=halo_send.at[2 * layer + 1],
            recv_sem=halo_recv.at[2 * layer + 1],
            device_id={"seq": seq - 1},
            device_id_type=MESH,
        )

    def send_right(layer):
        @pl.when(seq < seq_count - 1)
        def _():
            to_right(layer).start()

    def send_left(layer):
        @pl.when(seq > 0)
        def _():
            to_left(layer).start()

    def wait_left_rim(layer):
        @pl.when(seq > 0)
        def _():
            to_right(layer).wait_recv()

    def wait_right_rim(layer):
        @pl.when(seq < seq_count - 1)
        def _():
            to_left(layer).wait_recv()

    def mid_copy(which):
        return pltpu.make_async_remote_copy(
            src_ref=mids.at[me, which],
            dst_ref=mids.at[me, which],
            send_sem=mid_sem.at[which],
            recv_sem=mid_sem.at[2 + which],
            device_id={"chan": other},
            device_id_type=MESH,
        )

    def part_copy(layer, c):
        return pltpu.make_async_remote_copy(
            src_ref=sent.at[layer, pl.ds(c * step, step)],
            dst_ref=got.at[layer, pl.ds(c * step, step)],
            send_sem=part_send.at[CHUNKS * layer + c],
            recv_sem=part_recv.at[CHUNKS * layer + c],
            device_id={"chan": other},
            device_id_type=MESH,
        )

    def diff_copy(c):
        return pltpu.make_async_remote_copy(
            src_ref=diff_sent.at[pl.ds(c * half, half)],
            dst_ref=diff_got.at[pl.ds(c * half, half)],
            send_sem=diff_send.at[c],
            recv_sem=diff_recv.at[c],
            device_id={"chan": other},
            device_id_type=MESH,
        )

    places = bases.shape[0]
    columns = 4 * places
    spread = (
        lax.broadcasted_iota(jnp.int32, (places, columns), 1) // 4
        == lax.broadcasted_iota(jnp.int32, (places, columns), 0)
    ).astype(F32).astype(BF16)
    code = (lax.broadcasted_iota(jnp.int32, (1, columns), 1) % 4).astype(F32)

    def activate(layer, value):
        return gelu(
            value.astype(F32) * scale[layer : layer + 1, :] + shift[layer : layer + 1, :]
        ).astype(BF16)

    def start(c):
        at = pl.ds(c * step, step)
        repeated = lax.dot_general(
            bases[:, at].astype(F32).astype(BF16),
            spread,
            (((0,), (0,)), ((), ())),
            preferred_element_type=F32,
        )
        onehot = jnp.where(repeated == code, 1.0, 0.0).astype(BF16)
        value = (tower[at].astype(F32) + dot(onehot, embed[...])).astype(BF16)
        stream[at] = value
        padded0[pl.ds(PAD + c * step, step)] = activate(0, value)

    def convolve(layer, c):
        d = SPACINGS[layer]
        base = PAD + c * step
        taps = jnp.concatenate(
            [padded[layer][pl.ds(base + k * d, step)] for k in (-1, 0, 1)], axis=1
        )
        sent[layer, pl.ds(c * step, step)] = dot(taps, conv[layer]).astype(BF16)

    def pairs(c):
        return tuple(
            jnp.concatenate(
                [final[j, pl.ds(c * step + r, half, stride=2)] for j in range(width // LANES)], axis=1
            )
            for r in range(2)
        )

    def finish(layer, c):
        at = pl.ds(c * step, step)
        total = sent[layer, at].astype(F32) + got[layer, at].astype(F32)
        gain = jnp.concatenate([mids[0, 0, layer : layer + 1], mids[1, 0, layer : layer + 1]], axis=1)
        bias = jnp.concatenate([mids[0, 1, layer : layer + 1], mids[1, 1, layer : layer + 1]], axis=1)
        inner = gelu(total * gain + bias).astype(BF16)
        value = stream[at].astype(F32) + dot(inner, point[layer])
        if layer == 0:
            value = value.astype(BF16)
            stream[at] = value
            padded1[pl.ds(PAD + c * step, step)] = activate(1, value)
        else:
            for j in range(width // LANES):
                final[j, at] = value[:, j * LANES : (j + 1) * LANES]
            even, odd = pairs(c)
            diff_sent[pl.ds(c * half, half)] = (even - odd).astype(BF16)

    def emit(c):
        at = pl.ds(c * half, half)
        logits = dot(diff_sent[at], pool[0])
        logits = logits + dot(diff_got[at], pool[1])
        weigh = 0.5 + 0.5 * jnp.tanh(0.5 * logits)
        even, odd = pairs(c)
        out[at] = (odd + weigh * (even - odd)).astype(BF16)

    def together(conv_at=None, finish_at=None, emit_at=None):
        if finish_at is not None:
            part_copy(*finish_at).wait_recv()
        if emit_at is not None:
            diff_copy(emit_at).wait_recv()
        if conv_at is not None:
            convolve(*conv_at)
        if emit_at is not None:
            emit(emit_at)
        if finish_at is not None:
            finish(*finish_at)
        if conv_at is not None:
            part_copy(*conv_at).start()
        if finish_at is not None and finish_at[0] == 1:
            diff_copy(finish_at[1]).start()

    for name in ("bases", "embed", "tower", "scale", "shift"):
        loads[name].wait()
    load_block(0)
    last = CHUNKS - 1
    start(0)
    start(last)
    pl.semaphore_wait(
        barrier,
        1 + jnp.where(seq > 0, 1, 0) + jnp.where(seq < seq_count - 1, 1, 0),
    )
    send_left(0)
    send_right(0)
    for which in range(2):
        loads["mid%d" % which].wait()
        mid_copy(which).start()
    for c in range(1, last):
        start(c)

    for tap in range(3):
        loads[("conv", 0, tap)].wait()
    load_block(1)
    load("pool0", pool_h.at[pl.ds(pl.multiple_of(me * width, width), width)], pool.at[0], load_sem.at[9])
    load("pool1", pool_h.at[pl.ds(pl.multiple_of(other * width, width), width)], pool.at[1], load_sem.at[10])
    together(conv_at=(0, 1))
    together(conv_at=(0, 2))
    loads[("point", 0)].wait()
    for which in range(2):
        mid_copy(which).wait_recv()
    wait_left_rim(0)
    together(conv_at=(0, 0), finish_at=(0, 1))
    wait_right_rim(0)
    together(conv_at=(0, 3), finish_at=(0, 2))
    together(finish_at=(0, 0))
    send_left(1)
    for tap in range(3):
        loads[("conv", 1, tap)].wait()
    together(conv_at=(1, 1), finish_at=(0, 3))
    send_right(1)
    together(conv_at=(1, 2))
    loads[("point", 1)].wait()
    wait_right_rim(1)
    together(conv_at=(1, 3), finish_at=(1, 1))
    loads["pool0"].wait()
    loads["pool1"].wait()
    wait_left_rim(1)
    together(conv_at=(1, 0), finish_at=(1, 2))
    together(finish_at=(1, 3), emit_at=1)
    together(finish_at=(1, 0), emit_at=2)
    together(emit_at=3)
    together(emit_at=0)

    for layer in range(2):
        @pl.when(seq < seq_count - 1)
        def _():
            to_right(layer).wait_send()

        @pl.when(seq > 0)
        def _():
            to_left(layer).wait_send()

        mid_copy(layer).wait_send()
        for c in range(CHUNKS):
            part_copy(layer, c).wait_send()
    for c in range(CHUNKS):
        diff_copy(c).wait_send()


def local(seq_count, tower_input, dna_bases, base_embed, in_scale, entry_norm_shift, conv_w, mid_scale, mid_shift, point_w, pooling_weight):
    rows, width = tower_input.shape
    inner = point_w.shape[1]
    anywhere = pl.BlockSpec(memory_space=pl.ANY)
    dma = pltpu.SemaphoreType.DMA
    return pl.pallas_call(
        functools.partial(kernel, seq_count),
        out_shape=pltpu.VMEM((rows // 2, width), BF16),
        in_specs=[anywhere] * 10,
        out_specs=pl.BlockSpec(memory_space=pltpu.VMEM),
        scratch_shapes=[
            pltpu.VMEM((rows, width), BF16),
            pltpu.VMEM(dna_bases.shape[::-1], jnp.int32),
            pltpu.VMEM(base_embed.shape, BF16),
            pltpu.VMEM(in_scale.shape, F32),
            pltpu.VMEM(entry_norm_shift.shape, F32),
            pltpu.VMEM((2, 3 * width, inner), BF16),
            pltpu.VMEM((2, 2) + mid_scale.shape, F32),
            pltpu.VMEM(point_w.shape, BF16),
            pltpu.VMEM((2, width, width), BF16),
            pltpu.VMEM((rows, width), BF16),
            pltpu.VMEM((rows + 2 * PAD, width), BF16),
            pltpu.VMEM((rows + 2 * PAD, width), BF16),
            pltpu.VMEM((2, rows, inner), BF16),
            pltpu.VMEM((2, rows, inner), BF16),
            pltpu.VMEM((width // LANES, rows, LANES), F32),
            pltpu.VMEM((rows // 2, width), BF16),
            pltpu.VMEM((rows // 2, width), BF16),
            dma((11,)),
            dma((6,)),
            dma((4,)),
            dma((4,)),
            dma((4,)),
            dma((2 * CHUNKS,)),
            dma((2 * CHUNKS,)),
            dma((CHUNKS,)),
            dma((CHUNKS,)),
        ],
        compiler_params=pltpu.CompilerParams(
            collective_id=0, has_side_effects=True, vmem_limit_bytes=56 * 1024 * 1024
        ),
    )(tower_input, dna_bases.T, base_embed, in_scale, entry_norm_shift, conv_w, mid_scale, mid_shift, point_w, pooling_weight)


def solution(mesh):
    return jax.shard_map(
        functools.partial(local, mesh.shape["seq"]),
        mesh=mesh,
        in_specs=(
            P(("groups", "seq"), "chan"),
            P(("groups", "seq"), None),
            P(None, "chan"),
            P(None, "chan"),
            P(None, "chan"),
            P(None, None, "chan", None),
            P(None, "chan"),
            P(None, "chan"),
            P(None, None, "chan"),
            P(None, "chan"),
        ),
        out_specs=P(("groups", "seq"), "chan"),
        check_vma=False,
    )
```
